32 devices in a mesh: groups: 2 (over y), blk: 4 (over z), cells: 2 (over x), rep: 2 (over core).
Axes of the slice: x: 2, y: 2, z: 4, core: 2. Of those that a mesh axis runs over, the one named last changes fastest.
Arguments:
- probes: bfloat16 [32, 2, 4096], P('rep', 'cells', ('groups', 'blk')), parts along dimension 2, may hold values from -6 to 6
- depth_level: int32 [2, 4096], P('cells', ('groups', 'blk')), parts along dimension 1, may hold values from 0 to 15
- depth_scale: float32 [16], replicated, may hold values from 0.2 to 1.5
- sensitivity: bfloat16 [6, 3072, 2, 2048], P(None, ('groups', 'blk'), 'cells'), parts along dimension 1, may hold values from -0.125 to 0.125
- data_weight: float32 [6, 3072], P(None, ('groups', 'blk')), parts along dimension 1, may hold values from 0.05 to 0.5
- face_first: int32 [2, 2048], P('cells', ('groups', 'blk')), parts along dimension 1, may hold values from 0 to 2047, as said below
- face_second: int32 [2, 2048], P('cells', ('groups', 'blk')), parts along dimension 1, may hold values from 0 to 4095, as said below
- face_coef: float32 [2, 2048], P('cells', ('groups', 'blk')), parts along dimension 1, may hold values from 0.2 to 0.8
- face_count: int32 [2, 8], P('cells', ('groups', 'blk')), parts along dimension 1, may hold values from 51 to 256, as said below
Outputs:
- hessian_probe: float32 [32, 2, 4096], P('rep', 'cells', ('groups', 'blk')), parts along dimension 2
The draws below stay inside these ranges and needn't reach their ends.
There are 2 independent parts, one for each index of `groups`. The reference program is written for one: setup_inputs(seed, part) draws one part's arguments, and reference() takes and returns one part's arrays. A program takes and returns all parts, laid end to end along the dimension named above; an argument that names none is the same for every part. Nothing has to cross between parts.
Inputs may be any that keep to these rules, and one draw needn't show every extreme that they name: `face_first`: a cell number within partition p. `face_second`: never equal to face_first of the same slot; values of 2048 or more name cells of the next partition, which the last partition never does. Only the first face_count[p, b] slots of block b of partition p (slots b * 256 onward) hold faces, the others are ignored; in every draw some block is full.
All inputs are finite; a program needn't handle non-finite values.
Results may differ from the reference program's by a relative error of at most 0.0029.
Values may be sent and summed in bfloat16 or wider, within the bound.
A program may use at most 64 MiB of HBM per device.

```python
import math
import jax
import jax.numpy as jnp
from jax import lax

COMPS = 6
CELLS = 4096
PROBES = 32
LEVELS = 16
FACE_DEV = 256
STATIONS = 1536
NPART = 2
CP = 2048
FACES = 1024
BLOCKS = 4


def face_pairs(key):
    first_cell = jax.random.randint(jax.random.fold_in(key, 11), (NPART, FACES), 0, CP)
    shift_own = jax.random.randint(jax.random.fold_in(key, 12), (NPART, FACES), 1, 2 * CP)
    shift_last = jax.random.randint(jax.random.fold_in(key, 13), (NPART, FACES), 1, CP)
    last_part = jnp.arange(NPART)[:, None] == NPART - 1
    second_cell = jnp.where(last_part, (first_cell + shift_last) % CP, (first_cell + shift_own) % (2 * CP))
    return (first_cell.astype(jnp.int32), second_cell.astype(jnp.int32))


def draw_face_first(key, part):
    return face_pairs(key)[0]


def draw_face_second(key, part):
    return face_pairs(key)[1]


def draw_face_count(key, part):
    counts = jax.random.randint(jax.random.fold_in(key, 21), (NPART * BLOCKS,), FACE_DEV // 5, FACE_DEV + 1)
    full_block = jax.random.randint(jax.random.fold_in(key, 22), (), 0, NPART * BLOCKS)
    flat_counts = jnp.where(jnp.arange(NPART * BLOCKS) == full_block, FACE_DEV, counts)
    return flat_counts.reshape(NPART, BLOCKS).astype(jnp.int32)


def plant(array, key, smallest, top_value):
    place = [jax.random.randint(jax.random.fold_in(key, axis), (), 0, length) for axis, length in enumerate(array.shape)]
    main_axis = array.shape.index(max(array.shape))
    next_to = place[:main_axis] + [(place[main_axis] + 1) % array.shape[main_axis]] + place[main_axis + 1:]
    return array.at[tuple(place)].set(smallest).at[tuple(next_to)].set(top_value)


def strengthened(entries, own_key, source, target, blocks, factor):
    def block_of(axis_at):
        return (jnp.arange(entries.shape[axis_at]) // (entries.shape[axis_at] // blocks)).reshape((-1,) + (1,) * (entries.ndim - 1 - axis_at))

    first = jax.random.permutation(own_key, blocks)[block_of(target)]
    other_side = (block_of(target) + blocks // 2) % blocks
    return jnp.where((block_of(source) == first) | (block_of(source) == other_side), factor * entries, entries)


def level_of(key, extent, pieces, smallest, high):
    def one(axis_at, shards_of):
        steps = jax.random.uniform(jax.random.fold_in(jax.random.fold_in(key, 6), axis_at), (shards_of,), jnp.float32, smallest / len(pieces), high / len(pieces))
        return jnp.repeat(jnp.exp(steps), extent[axis_at] // shards_of).reshape((-1,) + (1,) * (len(extent) - axis_at - 1))

    gain = one(*pieces[0])
    for cut in pieces[1:]:
        gain = gain * one(*cut)
    return gain


def noise(rng, extent, scale, most, pieces=(), kind=jnp.bfloat16):
    loudness = level_of(rng, extent, pieces, -0.22, 0.18) if pieces else 1.0
    array = jax.random.normal(rng, extent, jnp.float32) * scale * loudness
    return jnp.minimum(jnp.maximum(array, -most), most).astype(kind)


def noise_with(key, shape, scale, reach, cuts, heavy, held_as=jnp.bfloat16):
    drawn = scale * jax.random.normal(key, shape, jnp.float32)
    if cuts:
        drawn = drawn * level_of(key, shape, cuts, -0.22, 0.18)
    return jnp.clip(strengthened(drawn, jax.random.fold_in(key, 3), *heavy), -reach, reach).astype(held_as)


def setup_inputs(seed: int = 0, part: int = 0) -> dict:
    splits = jax.random.split(jax.random.key(seed), 10)
    part_splits = jax.random.split(jax.random.fold_in(splits[9], part), 10)
    probes = noise(part_splits[0], (PROBES, NPART, CP), 1.0, 6.0, ((0, 2), (1, 2), (2, 4)))
    depth_level = plant(jax.random.randint(part_splits[1], (NPART, CP), 0, LEVELS), jax.random.fold_in(part_splits[1], 1), 0, LEVELS - 1).astype(jnp.int32)
    depth_scale = jnp.clip(jnp.exp(jax.random.uniform(splits[2], (LEVELS,), jnp.float32, math.log(0.2), math.log(1.5))), 0.2, 1.5)
    sensitivity = noise_with(part_splits[3], (COMPS, STATIONS, NPART, CP), CELLS ** -0.5, 0.125, ((1, 4), (2, 2)), (1, 3, 4, 2.0))
    data_weight = jnp.clip(jnp.exp(math.log(0.5) - 2.3025851 * jax.random.uniform(part_splits[4], (COMPS, STATIONS), jnp.float32) ** level_of(part_splits[4], (COMPS, STATIONS), ((1, 4),), -0.2, 0.2)), 0.05, 0.5)
    face_first = draw_face_first(jax.random.fold_in(jax.random.fold_in(splits[9], part), 71), part)
    face_second = draw_face_second(jax.random.fold_in(jax.random.fold_in(splits[9], part), 71), part)
    face_coef = jnp.clip(jnp.exp(math.log(0.8) - 1.3862944 * jax.random.uniform(part_splits[7], (NPART, FACES), jnp.float32) ** level_of(part_splits[7], (NPART, FACES), ((0, 2), (1, 4)), -0.2, 0.2)), 0.2, 0.8)
    face_count = draw_face_count(jax.random.fold_in(jax.random.fold_in(splits[9], part), 71), part)
    return {"probes": probes, "depth_level": depth_level, "depth_scale": depth_scale, "sensitivity": sensitivity, "data_weight": data_weight, "face_first": face_first, "face_second": face_second, "face_coef": face_coef, "face_count": face_count}


def reference(probes, depth_level, depth_scale, sensitivity, data_weight, face_first, face_second, face_coef, face_count):
    depth_factor = depth_scale[depth_level]
    weighted = (probes.astype(jnp.float32) * depth_factor[None]).astype(jnp.bfloat16)
    weighted_f = weighted.astype(jnp.float32)

    def component(comp_index):
        sens_comp = lax.dynamic_index_in_dim(sensitivity, comp_index, 0, keepdims=False).astype(jnp.float32)
        part_sums = jnp.einsum("spc,qpc->pqs", sens_comp, weighted_f)
        predicted = jnp.sum(part_sums, axis=0)
        weight_row = lax.dynamic_index_in_dim(data_weight, comp_index, 0, keepdims=False)
        residual = (weight_row[None] * predicted).astype(jnp.bfloat16)
        return jnp.einsum("spc,qs->qpc", sens_comp, residual.astype(jnp.float32))

    adjoint = jnp.sum(lax.map(component, jnp.arange(COMPS, dtype=jnp.int32)), axis=0)

    part_base = (jnp.arange(NPART, dtype=jnp.int32) * CP)[:, None]
    first_cell = (part_base + face_first).reshape(-1)
    second_cell = (part_base + face_second).reshape(-1)
    slot_index = jnp.arange(FACES, dtype=jnp.int32) % FACE_DEV
    slot_owner = jnp.arange(FACES, dtype=jnp.int32) // FACE_DEV
    live_slots = (slot_index[None, :] < face_count[:, slot_owner]).astype(jnp.float32).reshape(-1)
    flat_cells = weighted_f.reshape(PROBES, CELLS)
    coef_flat = face_coef.reshape(-1)
    jump_term = coef_flat * live_slots * (flat_cells[:, first_cell] - flat_cells[:, second_cell])
    flux_term = coef_flat * jump_term
    smooth = jnp.zeros((PROBES, CELLS), jnp.float32)
    smooth = smooth.at[:, first_cell].add(flux_term).at[:, second_cell].add(-flux_term)
    return depth_factor[None] * (adjoint + smooth.reshape(PROBES, NPART, CP))
```

```python
import functools

import jax
import jax.numpy as jnp
from jax import lax
from jax.experimental import pallas as pl
from jax.experimental.pallas import tpu as pltpu
from jax.sharding import PartitionSpec as P

CHUNKS = 3
BUILD_ROWS = 256
MESH = pl.DeviceIdType.MESH


def shifted(block, axis, distance):
    devices = range(lax.axis_size(axis))
    route = [(i - distance, i) for i in devices if i - distance in devices]
    return lax.ppermute(block, axis, route)


def level_scale(depth_level, depth_scale):
    levels = jnp.arange(depth_scale.shape[0], dtype=jnp.int32)
    pick_rows = (depth_level[..., None] == levels).astype(jnp.float32)
    return jnp.sum(pick_rows * depth_scale, axis=-1)


def pick_hot(indices, offset, count):
    return (indices[:, None] - offset == jnp.arange(count, dtype=jnp.int32)[None, :]).astype(
        jnp.bfloat16
    )


def pick_values(block, hot):
    dims = (((1,), (1,)), ((), ()))
    return lax.dot_general(block, hot, dims, preferred_element_type=jnp.float32)


def spread_flux(flux, hot):
    upper = flux.astype(jnp.bfloat16)
    lower = (flux - upper.astype(jnp.float32)).astype(jnp.bfloat16)
    return jnp.dot(upper, hot, preferred_element_type=jnp.float32) + jnp.dot(
        lower, hot, preferred_element_type=jnp.float32
    )


def plain_form(
    probes,
    depth_level,
    depth_scale,
    sensitivity,
    data_weight,
    face_first,
    face_second,
    face_coef,
    face_count,
):
    own_scale = level_scale(depth_level, depth_scale)
    weighted = (probes.astype(jnp.float32) * own_scale[None]).astype(jnp.bfloat16)
    probe_block = lax.all_gather(weighted, "blk", axis=2, tiled=True)
    slot_count = face_first.shape[1]
    live_all = (jnp.arange(slot_count, dtype=jnp.int32) < face_count[0, 0]).astype(jnp.float32)
    matrix = sensitivity[:, :, 0, :]
    first_cell = face_first[0]
    second_cell = face_second[0]
    coef_slots = face_coef[0]
    probe_cols = probe_block[:, 0, :]
    part_cells = probe_cols.shape[1]
    partial_value = jnp.einsum(
        "msc,qc->qms", matrix, probe_cols, preferred_element_type=jnp.float32
    )
    predicted = lax.psum(partial_value, "cells")
    residual = (data_weight[None] * predicted).astype(jnp.bfloat16)
    adjoint = jnp.einsum("msc,qms->qc", matrix, residual, preferred_element_type=jnp.float32)
    first_hot = pick_hot(first_cell, 0, part_cells)
    second_own = pick_hot(second_cell, 0, part_cells)
    first_val = pick_values(probe_cols, first_hot)
    second_val = pick_values(probe_cols, second_own)
    crossing = (second_cell >= part_cells).astype(jnp.float32)
    asked = shifted(second_cell, "cells", 1)
    asked_hot = pick_hot(asked, part_cells, part_cells)
    answer = pick_values(probe_cols, asked_hot).astype(jnp.bfloat16)
    received = shifted(answer, "cells", -1)
    second_val = second_val + crossing * received.astype(jnp.float32)
    flux_term = coef_slots * (coef_slots * live_all * (first_val - second_val))
    own_term = spread_flux(flux_term, first_hot) - spread_flux(flux_term, second_own)
    sent_flux = shifted(flux_term * crossing, "cells", 1)
    arrived = -spread_flux(sent_flux, asked_hot)
    total_term = (adjoint + own_term + arrived)[:, None, :]
    result = lax.psum_scatter(total_term, "blk", scatter_dimension=2, tiled=True)
    return result * own_scale[None]


NN = (((1,), (0,)), ((), ()))
NT = (((1,), (1,)), ((), ()))


def mxu(left, right, dims=NN):
    return lax.dot_general(left, right, dims, preferred_element_type=jnp.float32)


def in_two(value):
    upper = value.astype(jnp.bfloat16)
    lower = (value - upper.astype(jnp.float32)).astype(jnp.bfloat16)
    return jnp.concatenate([upper, lower], axis=0)


def fused_kernel(
    nblk,
    probes,
    level,
    table,
    sens,
    weight,
    first,
    second,
    coef,
    count,
    out,
    s_buf,
    w_buf,
    hot,
    asked,
    ans_send,
    ans_recv,
    flux_send,
    flux_recv,
    p_own,
    p_send,
    p_recv,
    acc,
    part_send,
    part_recv,
    load_sem,
    ask_sem,
    gather_sem,
    ans_sem,
    flux_sem,
    p_sem,
    part_sem,
):
    blk = lax.axis_index("blk")
    other = 1 - lax.axis_index("cells")
    probe_count, own_cells = probes.shape
    part_cells = w_buf.shape[1]
    slots = first.shape[1]
    chunk_rows = s_buf.shape[0] // CHUNKS
    comps, stations = weight.shape
    per_chunk = comps // CHUNKS

    def block(index):
        return pl.ds(pl.multiple_of(index * own_cells, own_cells), own_cells)

    def rows(k):
        return pl.ds(k * chunk_rows, chunk_rows)

    def to_blk(src, dst, sem, d):
        return pltpu.make_async_remote_copy(
            src_ref=src,
            dst_ref=dst,
            send_sem=sem.at[0, d - 1],
            recv_sem=sem.at[1, d - 1],
            device_id={"blk": lax.rem(blk + d, nblk)},
            device_id_type=MESH,
        )

    def to_other(src, dst, sem, k=0):
        return pltpu.make_async_remote_copy(
            src_ref=src,
            dst_ref=dst,
            send_sem=sem.at[0, k],
            recv_sem=sem.at[1, k],
            device_id={"cells": other},
            device_id_type=MESH,
        )

    barrier = pltpu.get_barrier_semaphore()
    for d in range(1, nblk):
        pl.semaphore_signal(
            barrier, inc=1, device_id={"blk": lax.rem(blk + d, nblk)}, device_id_type=MESH
        )
    pl.semaphore_signal(barrier, inc=1, device_id={"cells": other}, device_id_type=MESH)

    loads = [
        pltpu.make_async_copy(sens.at[rows(k), :], s_buf.at[rows(k), :], load_sem.at[k])
        for k in range(CHUNKS)
    ]
    for load in loads:
        load.start()

    levels = level[...]
    scale = jnp.zeros(levels.shape, jnp.float32)
    for index in range(table.shape[0]):
        scale = jnp.where(levels == index, table[index], scale)
    weighted = (probes[...].astype(jnp.float32) * scale).astype(jnp.bfloat16)
    w_buf[:, block(blk)] = weighted

    pl.semaphore_wait(barrier, nblk)
    gathers = [
        to_blk(w_buf.at[:, block(blk)], w_buf.at[:, block(blk)], gather_sem, d)
        for d in range(1, nblk)
    ]
    for copy in gathers:
        copy.start()
    ask = to_other(second, asked, ask_sem)
    ask.start()

    first_row = first[...]
    second_row = second[...]
    cell_in = lax.broadcasted_iota(jnp.int32, (BUILD_ROWS, slots), 0)

    def build_own(step, carry):
        base = pl.multiple_of(step * BUILD_ROWS, BUILD_ROWS)
        one = jnp.where(cell_in == first_row - base, 1.0, 0.0)
        both = jnp.where(cell_in == second_row - base, -1.0, one)
        hot[pl.ds(base, BUILD_ROWS), pl.ds(0, slots)] = both.astype(jnp.bfloat16)
        return carry

    lax.fori_loop(0, part_cells // BUILD_ROWS, build_own, 0)
    ask.wait_recv()
    asked_row = asked[...] - part_cells

    def build_asked(step, carry):
        base = pl.multiple_of(step * BUILD_ROWS, BUILD_ROWS)
        one = jnp.where(cell_in == asked_row - base, 1.0, 0.0)
        hot[pl.ds(base, BUILD_ROWS), pl.ds(slots, slots)] = one.astype(jnp.bfloat16)
        return carry

    lax.fori_loop(0, part_cells // BUILD_ROWS, build_asked, 0)

    for copy in gathers:
        copy.wait_recv()
    cols = w_buf[...]
    ans_send[...] = mxu(cols, hot[:, slots:]).astype(jnp.bfloat16)
    answer = to_other(ans_send, ans_recv, ans_sem)
    answer.start()

    swaps = []
    for k in range(CHUNKS):
        loads[k].wait()
        partial = mxu(cols, s_buf[rows(k), :], NT)
        p_own[:, rows(k)] = partial
        p_send[k] = partial.astype(jnp.bfloat16)
        swap = to_other(p_send.at[k], p_recv.at[k], p_sem, k)
        swap.start()
        swaps.append(swap)

    jump = mxu(cols, hot[:, :slots])
    crossing = jnp.where(second_row >= part_cells, 1.0, 0.0)
    live = jnp.where(lax.broadcasted_iota(jnp.int32, (1, slots), 1) < count[0, 0], 1.0, 0.0)
    coef_row = coef[...]
    answer.wait_recv()
    jump = jump - crossing * ans_recv[...].astype(jnp.float32)
    flux = coef_row * (coef_row * live * jump)
    flux_send[...] = -(flux * crossing)
    forward = to_other(flux_send, flux_recv, flux_sem)
    forward.start()
    flux_pair = in_two(flux)

    def residual_of(k):
        predicted = p_own[:, rows(k)] + p_recv[k].astype(jnp.float32)
        factor = jnp.concatenate(
            [weight[pl.ds(k * per_chunk + i, 1), :] for i in range(per_chunk)], axis=1
        )
        return (factor * predicted).astype(jnp.bfloat16)

    for k in range(CHUNKS - 1):
        swaps[k].wait_recv()
        term = mxu(residual_of(k), s_buf[rows(k), :])
        if k == 0:
            acc[...] = term
        else:
            acc[...] += term

    forward.wait_recv()
    pairs = jnp.concatenate([flux_pair, in_two(flux_recv[...])], axis=1)
    swaps[-1].wait_recv()
    last = residual_of(CHUNKS - 1)
    sums = []
    total = None
    for d in list(range(1, nblk)) + [0]:
        here = block(lax.rem(blk + d, nblk))
        spread = mxu(pairs, hot[here, :], NT)
        term = (
            acc[:, here]
            + mxu(last, s_buf[rows(CHUNKS - 1), here])
            + (spread[:probe_count] + spread[probe_count:])
        )
        if d:
            part_send[d - 1] = term.astype(jnp.bfloat16)
            copy = to_blk(part_send.at[d - 1], part_recv.at[d - 1], part_sem, d)
            copy.start()
            sums.append(copy)
        else:
            total = term
    for d in range(1, nblk):
        sums[d - 1].wait_recv()
        total = total + part_recv[d - 1].astype(jnp.float32)
    out[...] = total * scale

    for copy in gathers + [ask, answer, forward] + swaps + sums:
        copy.wait_send()


def fused_form(
    nblk,
    probes,
    depth_level,
    depth_scale,
    sensitivity,
    data_weight,
    face_first,
    face_second,
    face_coef,
    face_count,
):
    probe_count, _, own_cells = probes.shape
    comps, stations, _, part_cells = sensitivity.shape
    rows = comps * stations
    slots = face_first.shape[1]
    matrix = sensitivity[:, :, 0, :].reshape(rows, part_cells)
    vmem = pl.BlockSpec(memory_space=pltpu.VMEM)
    smem = pl.BlockSpec(memory_space=pltpu.SMEM)
    bf16, f32 = jnp.bfloat16, jnp.float32
    dma = pltpu.SemaphoreType.DMA
    result = pl.pallas_call(
        functools.partial(fused_kernel, nblk),
        out_shape=jax.ShapeDtypeStruct((probe_count, own_cells), f32),
        in_specs=[
            vmem,
            vmem,
            smem,
            pl.BlockSpec(memory_space=pl.ANY),
            vmem,
            vmem,
            vmem,
            vmem,
            smem,
        ],
        out_specs=vmem,
        scratch_shapes=[
            pltpu.VMEM((rows, part_cells), bf16),
            pltpu.VMEM((probe_count, part_cells), bf16),
            pltpu.VMEM((part_cells, 2 * slots), bf16),
            pltpu.VMEM((1, slots), jnp.int32),
            pltpu.VMEM((probe_count, slots), bf16),
            pltpu.VMEM((probe_count, slots), bf16),
            pltpu.VMEM((probe_count, slots), f32),
            pltpu.VMEM((probe_count, slots), f32),
            pltpu.VMEM((probe_count, rows), f32),
            pltpu.VMEM((CHUNKS, probe_count, rows // CHUNKS), bf16),
            pltpu.VMEM((CHUNKS, probe_count, rows // CHUNKS), bf16),
            pltpu.VMEM((probe_count, part_cells), f32),
            pltpu.VMEM((nblk - 1, probe_count, own_cells), bf16),
            pltpu.VMEM((nblk - 1, probe_count, own_cells), bf16),
            dma((CHUNKS,)),
            dma((2, 1)),
            dma((2, nblk - 1)),
            dma((2, 1)),
            dma((2, 1)),
            dma((2, CHUNKS)),
            dma((2, nblk - 1)),
        ],
        compiler_params=pltpu.CompilerParams(
            collective_id=0, has_side_effects=True, vmem_limit_bytes=56 * 2**20
        ),
        cost_estimate=pl.CostEstimate(
            flops=4 * probe_count * rows * part_cells,
            bytes_accessed=2 * rows * part_cells,
            transcendentals=0,
        ),
    )(
        probes[:, 0, :],
        depth_level,
        depth_scale,
        matrix,
        data_weight,
        face_first,
        face_second,
        face_coef,
        face_count,
    )
    return result[:, None, :]


def fits_kernel(nblk, ncells, probes, sensitivity):
    own_cells = probes.shape[2]
    comps, stations, _, part_cells = sensitivity.shape
    return (
        ncells == 2
        and own_cells % 128 == 0
        and part_cells % BUILD_ROWS == 0
        and stations % 128 == 0
        and comps % CHUNKS == 0
        and probes.shape[0] % 16 == 0
    )


def on_device(nblk, ncells, *arrays):
    if fits_kernel(nblk, ncells, arrays[0], arrays[3]):
        return fused_form(nblk, *arrays)
    return plain_form(*arrays)


def solution(mesh):
    return jax.shard_map(
        functools.partial(on_device, mesh.shape["blk"], mesh.shape["cells"]),
        mesh=mesh,
        in_specs=(
            P("rep", "cells", ("groups", "blk")),
            P("cells", ("groups", "blk")),
            P(),
            P(None, ("groups", "blk"), "cells", None),
            P(None, ("groups", "blk")),
            P("cells", ("groups", "blk")),
            P("cells", ("groups", "blk")),
            P("cells", ("groups", "blk")),
            P("cells", ("groups", "blk")),
        ),
        out_specs=P("rep", "cells", ("groups", "blk")),
        check_vma=False,
    )
```

```python
import functools

import jax
import jax.numpy as jnp
from jax import lax
from jax.experimental import pallas as pl
from jax.experimental.pallas import tpu as pltpu
from jax.sharding import PartitionSpec as P

CHUNKS = 3
BUILD_ROWS = 256
MESH = pl.DeviceIdType.MESH


def shifted(block, axis, distance):
    devices = range(lax.axis_size(axis))
    route = [(i - distance, i) for i in devices if i - distance in devices]
    return lax.ppermute(block, axis, route)


def level_scale(depth_level, depth_scale):
    levels = jnp.arange(depth_scale.shape[0], dtype=jnp.int32)
    pick_rows = (depth_level[..., None] == levels).astype(jnp.float32)
    return jnp.sum(pick_rows * depth_scale, axis=-1)


def pick_hot(indices, offset, count):
    return (indices[:, None] - offset == jnp.arange(count, dtype=jnp.int32)[None, :]).astype(
        jnp.bfloat16
    )


def pick_values(block, hot):
    dims = (((1,), (1,)), ((), ()))
    return lax.dot_general(block, hot, dims, preferred_element_type=jnp.float32)


def spread_flux(flux, hot):
    upper = flux.astype(jnp.bfloat16)
    lower = (flux - upper.astype(jnp.float32)).astype(jnp.bfloat16)
    return jnp.dot(upper, hot, preferred_element_type=jnp.float32) + jnp.dot(
        lower, hot, preferred_element_type=jnp.float32
    )


def plain_form(
    probes,
    depth_level,
    depth_scale,
    sensitivity,
    data_weight,
    face_first,
    face_second,
    face_coef,
    face_count,
):
    own_scale = level_scale(depth_level, depth_scale)
    weighted = (probes.astype(jnp.float32) * own_scale[None]).astype(jnp.bfloat16)
    probe_block = lax.all_gather(weighted, "blk", axis=2, tiled=True)
    slot_count = face_first.shape[1]
    live_all = (jnp.arange(slot_count, dtype=jnp.int32) < face_count[0, 0]).astype(jnp.float32)
    matrix = sensitivity[:, :, 0, :]
    first_cell = face_first[0]
    second_cell = face_second[0]
    coef_slots = face_coef[0]
    probe_cols = probe_block[:, 0, :]
    part_cells = probe_cols.shape[1]
    partial_value = jnp.einsum(
        "msc,qc->qms", matrix, probe_cols, preferred_element_type=jnp.float32
    )
    predicted = lax.psum(partial_value, "cells")
    residual = (data_weight[None] * predicted).astype(jnp.bfloat16)
    adjoint = jnp.einsum("msc,qms->qc", matrix, residual, preferred_element_type=jnp.float32)
    first_hot = pick_hot(first_cell, 0, part_cells)
    second_own = pick_hot(second_cell, 0, part_cells)
    first_val = pick_values(probe_cols, first_hot)
    second_val = pick_values(probe_cols, second_own)
    crossing = (second_cell >= part_cells).astype(jnp.float32)
    asked = shifted(second_cell, "cells", 1)
    asked_hot = pick_hot(asked, part_cells, part_cells)
    answer = pick_values(probe_cols, asked_hot).astype(jnp.bfloat16)
    received = shifted(answer, "cells", -1)
    second_val = second_val + crossing * received.astype(jnp.float32)
    flux_term = coef_slots * (coef_slots * live_all * (first_val - second_val))
    own_term = spread_flux(flux_term, first_hot) - spread_flux(flux_term, second_own)
    sent_flux = shifted(flux_term * crossing, "cells", 1)
    arrived = -spread_flux(sent_flux, asked_hot)
    total_term = (adjoint + own_term + arrived)[:, None, :]
    result = lax.psum_scatter(total_term, "blk", scatter_dimension=2, tiled=True)
    return result * own_scale[None]


NN = (((1,), (0,)), ((), ()))
NT = (((1,), (1,)), ((), ()))


def mxu(left, right, dims=NN):
    return lax.dot_general(left, right, dims, preferred_element_type=jnp.float32)


def in_two(value):
    upper = value.astype(jnp.bfloat16)
    lower = (value - upper.astype(jnp.float32)).astype(jnp.bfloat16)
    return jnp.concatenate([upper, lower], axis=0)


def fused_kernel(
    probes_in,
    level_in,
    table_in,
    sens,
    weight_in,
    first_in,
    second_in,
    coef_in,
    count_in,
    out,
    probes,
    level,
    table,
    weight,
    first,
    second,
    coef,
    count,
    s_buf,
    w_buf,
    hot,
    strength,
    asked,
    asked_strength,
    val_send,
    val_recv,
    val_own,
    p_own,
    p_send,
    p_recv,
    acc,
    part_send,
    part_recv,
    small_sem,
    load_sem,
    ask_sem,
    gather_sem,
    val_sem,
    p_sem,
    part_sem,
):
    nblk = 4
    blk = lax.axis_index("blk")
    other = 1 - lax.axis_index("cells")
    probe_count, own_cells = probes.shape
    part_cells = w_buf.shape[1]
    slots = first.shape[1]
    chunk_rows = s_buf.shape[0] // CHUNKS
    comps, stations = weight.shape
    per_chunk = comps // CHUNKS
    half = blk // 2

    def mirrored(place):
        return place + half * (nblk - 1 - 2 * place)

    peers = [mirrored(1 - mirrored(blk)), mirrored(2), mirrored(3)]

    def block(index):
        return pl.ds(pl.multiple_of(index * own_cells, own_cells), own_cells)

    def rows(k):
        return pl.ds(k * chunk_rows, chunk_rows)

    def to_blk(src, dst, sem, arrival, peer):
        return pltpu.make_async_remote_copy(
            src_ref=src,
            dst_ref=dst,
            send_sem=sem.at[0, peer],
            recv_sem=sem.at[1, arrival],
            device_id={"blk": peer},
            device_id_type=MESH,
        )

    def to_other(src, dst, sem, k=0):
        return pltpu.make_async_remote_copy(
            src_ref=src,
            dst_ref=dst,
            send_sem=sem.at[0, k],
            recv_sem=sem.at[1, k],
            device_id={"cells": other},
            device_id_type=MESH,
        )

    barrier = pltpu.get_barrier_semaphore()
    for peer in reversed(peers):
        pl.semaphore_signal(barrier, inc=1, device_id={"blk": peer}, device_id_type=MESH)
    pl.semaphore_signal(barrier, inc=1, device_id={"cells": other}, device_id_type=MESH)

    pairs_in = [
        (level_in, level),
        (table_in, table),
        (probes_in, probes),
        (first_in, first),
        (second_in, second),
        (coef_in, coef),
        (count_in, count),
        (weight_in, weight),
    ]
    smalls = [
        pltpu.make_async_copy(src, dst, small_sem.at[n]) for n, (src, dst) in enumerate(pairs_in)
    ]
    for copy in smalls:
        copy.start()
    loads = [
        pltpu.make_async_copy(sens.at[rows(k), :], s_buf.at[rows(k), :], load_sem.at[k])
        for k in range(CHUNKS)
    ]
    for copy in loads:
        copy.start()
    for copy in smalls:
        copy.wait()

    levels = level[...]
    scale = jnp.zeros(levels.shape, jnp.float32)
    for index in range(table.shape[0]):
        scale = jnp.where(levels == index, table[index], scale)
    weighted = (probes[...].astype(jnp.float32) * scale).astype(jnp.bfloat16)
    w_buf[:, block(blk)] = weighted
    live = lax.broadcasted_iota(jnp.int32, (1, slots), 1) < count[...]
    own_strength = jnp.where(live, coef[...], 0.0)
    strength[...] = own_strength

    pl.semaphore_wait(barrier, nblk)
    mine = w_buf.at[:, block(blk)]
    gathers = [to_blk(mine, mine, gather_sem, blk, peer) for peer in reversed(peers)]
    for copy in gathers:
        copy.start()
    asks = [to_other(second, asked, ask_sem, 0), to_other(strength, asked_strength, ask_sem, 1)]
    for copy in asks:
        copy.start()

    cell_in = lax.broadcasted_iota(jnp.int32, (BUILD_ROWS, slots), 0)

    def mark(cells, part):
        def build(step, carry):
            base = pl.multiple_of(step * BUILD_ROWS, BUILD_ROWS)
            one = jnp.where(cell_in == cells - base, 1.0, 0.0)
            hot[pl.ds(base, BUILD_ROWS), pl.ds(part * slots, slots)] = one.astype(jnp.bfloat16)
            return carry

        lax.fori_loop(0, part_cells // BUILD_ROWS, build, 0)

    second_row = second[...]
    mark(first[...], 0)
    mark(second_row, 1)
    for k in range(CHUNKS):
        loads[k].wait()
        p_own[:, rows(k)] = mxu(weighted, s_buf[rows(k), block(blk)], NT)
    for copy in asks:
        copy.wait_recv()
    mark(asked[...] - part_cells, 2)
    val_own[...] = mxu(weighted, hot[block(blk), :])

    swaps = []
    for place, peer in enumerate(peers):
        theirs = w_buf.at[:, block(peer)]
        to_blk(theirs, theirs, gather_sem, peer, peer).wait_recv()
        cols = w_buf[:, block(peer)]
        value = val_own[...] + mxu(cols, hot[block(peer), :])
        if place < nblk - 2:
            val_own[...] = value
        else:
            first_val = value[:, :slots]
            second_val = value[:, slots : 2 * slots]
            answer = value[:, 2 * slots :]
            val_send[...] = jnp.concatenate([first_val, answer], axis=1).astype(jnp.bfloat16)
            trade = to_other(val_send, val_recv, val_sem)
            trade.start()
        for k in range(CHUNKS):
            partial = p_own[:, rows(k)] + mxu(cols, s_buf[rows(k), block(peer)], NT)
            p_own[:, rows(k)] = partial
            if place == nblk - 2:
                p_send[k] = partial.astype(jnp.bfloat16)
                swap = to_other(p_send.at[k], p_recv.at[k], p_sem, k)
                swap.start()
                swaps.append(swap)

    def residual_of(k):
        predicted = p_own[:, rows(k)] + p_recv[k].astype(jnp.float32)
        factor = jnp.concatenate(
            [weight[pl.ds(k * per_chunk + i, 1), :] for i in range(per_chunk)], axis=1
        )
        return (factor * predicted).astype(jnp.bfloat16)

    crossing = jnp.where(second_row >= part_cells, 1.0, 0.0)
    trade.wait_recv()
    jump = first_val - second_val - crossing * val_recv[:, slots:].astype(jnp.float32)
    flux = own_strength * (own_strength * jump)
    far_strength = jnp.where(asked[...] >= part_cells, asked_strength[...], 0.0)
    far_jump = val_recv[:, :slots].astype(jnp.float32) - answer
    far_flux = far_strength * (far_strength * far_jump)
    flux_pair = in_two(jnp.concatenate([flux, -flux, -far_flux], axis=1))
    spread = mxu(flux_pair, hot[...], NT)
    spread = spread[:probe_count] + spread[probe_count:]
    swaps[0].wait_recv()
    acc[...] = spread + mxu(residual_of(0), s_buf[rows(0), :])

    for copy in swaps[1:]:
        copy.wait_recv()
    late = jnp.concatenate([residual_of(k) for k in range(1, CHUNKS)], axis=1)
    late_rows = pl.ds(chunk_rows, (CHUNKS - 1) * chunk_rows)
    sums = []
    for place, peer in enumerate(reversed(peers)):
        term = acc[:, block(peer)] + mxu(late, s_buf[late_rows, block(peer)])
        part_send[place] = term.astype(jnp.bfloat16)
        copy = to_blk(part_send.at[place], part_recv.at[blk], part_sem, blk, peer)
        copy.start()
        sums.append(copy)
    total = acc[:, block(blk)] + mxu(late, s_buf[late_rows, block(blk)])
    for peer in peers:
        theirs = part_recv.at[peer]
        to_blk(theirs, theirs, part_sem, peer, peer).wait_recv()
        total = total + part_recv[peer].astype(jnp.float32)
    out[...] = total * scale

    for copy in gathers + asks + [trade] + swaps + sums:
        copy.wait_send()


def hand_on(value, out):
    out[:, 0, :] = value[...]


def fused_form(
    nblk,
    probes,
    depth_level,
    depth_scale,
    sensitivity,
    data_weight,
    face_first,
    face_second,
    face_coef,
    face_count,
):
    probe_count, _, own_cells = probes.shape
    comps, stations, _, part_cells = sensitivity.shape
    rows = comps * stations
    slots = face_first.shape[1]
    matrix = sensitivity[:, :, 0, :].reshape(rows, part_cells)
    vmem = pl.BlockSpec(memory_space=pltpu.VMEM)
    bf16, f32, i32 = jnp.bfloat16, jnp.float32, jnp.int32
    dma = pltpu.SemaphoreType.DMA
    result = pl.pallas_call(
        fused_kernel,
        out_shape=jax.ShapeDtypeStruct((probe_count, own_cells), f32),
        in_specs=[pl.BlockSpec(memory_space=pl.ANY)] * 9,
        out_specs=vmem,
        scratch_shapes=[
            pltpu.VMEM((probe_count, own_cells), bf16),
            pltpu.VMEM((1, own_cells), i32),
            pltpu.SMEM(depth_scale.shape, f32),
            pltpu.VMEM((comps, stations), f32),
            pltpu.VMEM((1, slots), i32),
            pltpu.VMEM((1, slots), i32),
            pltpu.VMEM((1, slots), f32),
            pltpu.VMEM((1, 1), i32),
            pltpu.VMEM((rows, part_cells), bf16),
            pltpu.VMEM((probe_count, part_cells), bf16),
            pltpu.VMEM((part_cells, 3 * slots), bf16),
            pltpu.VMEM((1, slots), f32),
            pltpu.VMEM((1, slots), i32),
            pltpu.VMEM((1, slots), f32),
            pltpu.VMEM((probe_count, 2 * slots), bf16),
            pltpu.VMEM((probe_count, 2 * slots), bf16),
            pltpu.VMEM((probe_count, 3 * slots), f32),
            pltpu.VMEM((probe_count, rows), f32),
            pltpu.VMEM((CHUNKS, probe_count, rows // CHUNKS), bf16),
            pltpu.VMEM((CHUNKS, probe_count, rows // CHUNKS), bf16),
            pltpu.VMEM((probe_count, part_cells), f32),
            pltpu.VMEM((nblk - 1, probe_count, own_cells), bf16),
            pltpu.VMEM((nblk, probe_count, own_cells), bf16),
            dma((8,)),
            dma((CHUNKS,)),
            dma((2, 2)),
            dma((2, nblk)),
            dma((2, 1)),
            dma((2, CHUNKS)),
            dma((2, nblk)),
        ],
        compiler_params=pltpu.CompilerParams(
            collective_id=0, has_side_effects=True, vmem_limit_bytes=56 * 2**20
        ),
        cost_estimate=pl.CostEstimate(
            flops=4 * probe_count * rows * part_cells,
            bytes_accessed=2 * rows * part_cells,
            transcendentals=0,
        ),
    )(
        probes[:, 0, :],
        depth_level,
        depth_scale,
        matrix,
        data_weight,
        face_first,
        face_second,
        face_coef,
        face_count,
    )
    return pl.pallas_call(
        hand_on,
        out_shape=jax.ShapeDtypeStruct((probe_count, 1, own_cells), f32),
        in_specs=[vmem],
        out_specs=vmem,
    )(result)


def fits_kernel(nblk, ncells, probes, sensitivity):
    own_cells = probes.shape[2]
    comps, stations, _, part_cells = sensitivity.shape
    return (
        nblk == 4
        and ncells == 2
        and own_cells % 128 == 0
        and part_cells % BUILD_ROWS == 0
        and stations % 128 == 0
        and comps % CHUNKS == 0
        and probes.shape[0] % 16 == 0
    )


def on_device(nblk, ncells, *arrays):
    if fits_kernel(nblk, ncells, arrays[0], arrays[3]):
        return fused_form(nblk, *arrays)
    return plain_form(*arrays)


def solution(mesh):
    return jax.shard_map(
        functools.partial(on_device, mesh.shape["blk"], mesh.shape["cells"]),
        mesh=mesh,
        in_specs=(
            P("rep", "cells", ("groups", "blk")),
            P("cells", ("groups", "blk")),
            P(),
            P(None, ("groups", "blk"), "cells", None),
            P(None, ("groups", "blk")),
            P("cells", ("groups", "blk")),
            P("cells", ("groups", "blk")),
            P("cells", ("groups", "blk")),
            P("cells", ("groups", "blk")),
        ),
        out_specs=P("rep", "cells", ("groups", "blk")),
        check_vma=False,
    )
```

```python
import functools

import jax
import jax.numpy as jnp
from jax import lax
from jax.experimental import pallas as pl
from jax.experimental.pallas import tpu as pltpu
from jax.sharding import PartitionSpec as P

CHUNKS = 3
BUILD_ROWS = 256
MESH = pl.DeviceIdType.MESH


def shifted(block, axis, distance):
    devices = range(lax.axis_size(axis))
    route = [(i - distance, i) for i in devices if i - distance in devices]
    return lax.ppermute(block, axis, route)


def level_scale(depth_level, depth_scale):
    levels = jnp.arange(depth_scale.shape[0], dtype=jnp.int32)
    pick_rows = (depth_level[..., None] == levels).astype(jnp.float32)
    return jnp.sum(pick_rows * depth_scale, axis=-1)


def pick_hot(indices, offset, count):
    return (indices[:, None] - offset == jnp.arange(count, dtype=jnp.int32)[None, :]).astype(
        jnp.bfloat16
    )


def pick_values(block, hot):
    dims = (((1,), (1,)), ((), ()))
    return lax.dot_general(block, hot, dims, preferred_element_type=jnp.float32)


def spread_flux(flux, hot):
    upper = flux.astype(jnp.bfloat16)
    lower = (flux - upper.astype(jnp.float32)).astype(jnp.bfloat16)
    return jnp.dot(upper, hot, preferred_element_type=jnp.float32) + jnp.dot(
        lower, hot, preferred_element_type=jnp.float32
    )


def plain_form(
    probes,
    depth_level,
    depth_scale,
    sensitivity,
    data_weight,
    face_first,
    face_second,
    face_coef,
    face_count,
):
    own_scale = level_scale(depth_level, depth_scale)
    weighted = (probes.astype(jnp.float32) * own_scale[None]).astype(jnp.bfloat16)
    probe_block = lax.all_gather(weighted, "blk", axis=2, tiled=True)
    slot_count = face_first.shape[1]
    live_all = (jnp.arange(slot_count, dtype=jnp.int32) < face_count[0, 0]).astype(jnp.float32)
    matrix = sensitivity[:, :, 0, :]
    first_cell = face_first[0]
    second_cell = face_second[0]
    coef_slots = face_coef[0]
    probe_cols = probe_block[:, 0, :]
    part_cells = probe_cols.shape[1]
    partial_value = jnp.einsum(
        "msc,qc->qms", matrix, probe_cols, preferred_element_type=jnp.float32
    )
    predicted = lax.psum(partial_value, "cells")
    residual = (data_weight[None] * predicted).astype(jnp.bfloat16)
    adjoint = jnp.einsum("msc,qms->qc", matrix, residual, preferred_element_type=jnp.float32)
    first_hot = pick_hot(first_cell, 0, part_cells)
    second_own = pick_hot(second_cell, 0, part_cells)
    first_val = pick_values(probe_cols, first_hot)
    second_val = pick_values(probe_cols, second_own)
    crossing = (second_cell >= part_cells).astype(jnp.float32)
    asked = shifted(second_cell, "cells", 1)
    asked_hot = pick_hot(asked, part_cells, part_cells)
    answer = pick_values(probe_cols, asked_hot).astype(jnp.bfloat16)
    received = shifted(answer, "cells", -1)
    second_val = second_val + crossing * received.astype(jnp.float32)
    flux_term = coef_slots * (coef_slots * live_all * (first_val - second_val))
    own_term = spread_flux(flux_term, first_hot) - spread_flux(flux_term, second_own)
    sent_flux = shifted(flux_term * crossing, "cells", 1)
    arrived = -spread_flux(sent_flux, asked_hot)
    total_term = (adjoint + own_term + arrived)[:, None, :]
    result = lax.psum_scatter(total_term, "blk", scatter_dimension=2, tiled=True)
    return result * own_scale[None]


NN = (((1,), (0,)), ((), ()))
NT = (((1,), (1,)), ((), ()))


def mxu(left, right, dims=NN):
    return lax.dot_general(left, right, dims, preferred_element_type=jnp.float32)


def in_two(value):
    upper = value.astype(jnp.bfloat16)
    lower = (value - upper.astype(jnp.float32)).astype(jnp.bfloat16)
    return jnp.concatenate([upper, lower], axis=0)


def fused_kernel(
    probes_in,
    level_in,
    table_in,
    sens,
    weight_in,
    first_in,
    second_in,
    coef_in,
    count_in,
    out,
    probes,
    level,
    table,
    weight,
    first,
    second,
    coef,
    count,
    s_buf,
    w_buf,
    hot,
    strength,
    asked,
    asked_strength,
    val_send,
    val_recv,
    val_own,
    p_own,
    p_send,
    p_recv,
    acc,
    part_send,
    part_recv,
    small_sem,
    load_sem,
    ask_sem,
    gather_sem,
    val_sem,
    p_sem,
    part_sem,
):
    nblk = 4
    blk = lax.axis_index("blk")
    other = 1 - lax.axis_index("cells")
    probe_count, own_cells = probes.shape
    part_cells = w_buf.shape[1]
    slots = first.shape[1]
    chunk_rows = s_buf.shape[0] // CHUNKS
    comps, stations = weight.shape
    per_chunk = comps // CHUNKS
    half = blk // 2

    def mirrored(place):
        return place + half * (nblk - 1 - 2 * place)

    peers = [mirrored(1 - mirrored(blk)), mirrored(2), mirrored(3)]

    def block(index):
        return pl.ds(pl.multiple_of(index * own_cells, own_cells), own_cells)

    def rows(k):
        return pl.ds(k * chunk_rows, chunk_rows)

    def to_blk(src, dst, sem, arrival, peer):
        return pltpu.make_async_remote_copy(
            src_ref=src,
            dst_ref=dst,
            send_sem=sem.at[0, peer],
            recv_sem=sem.at[1, arrival],
            device_id={"blk": peer},
            device_id_type=MESH,
        )

    def to_other(src, dst, sem, k=0):
        return pltpu.make_async_remote_copy(
            src_ref=src,
            dst_ref=dst,
            send_sem=sem.at[0, k],
            recv_sem=sem.at[1, k],
            device_id={"cells": other},
            device_id_type=MESH,
        )

    barrier = pltpu.get_barrier_semaphore()
    for peer in reversed(peers):
        pl.semaphore_signal(barrier, inc=1, device_id={"blk": peer}, device_id_type=MESH)
    pl.semaphore_signal(barrier, inc=1, device_id={"cells": other}, device_id_type=MESH)

    pairs_in = [
        (level_in, level),
        (table_in, table),
        (probes_in, probes),
        (first_in, first),
        (second_in, second),
        (coef_in, coef),
        (count_in, count),
        (weight_in, weight),
    ]
    smalls = [
        pltpu.make_async_copy(src, dst, small_sem.at[n]) for n, (src, dst) in enumerate(pairs_in)
    ]
    for copy in smalls:
        copy.start()
    loads = [
        pltpu.make_async_copy(sens.at[rows(k), :], s_buf.at[rows(k), :], load_sem.at[k])
        for k in range(CHUNKS)
    ]
    for copy in loads:
        copy.start()
    for copy in smalls:
        copy.wait()

    levels = level[...]
    scale = jnp.zeros(levels.shape, jnp.float32)
    for index in range(table.shape[0]):
        scale = jnp.where(levels == index, table[index], scale)
    weighted = (probes[...].astype(jnp.float32) * scale).astype(jnp.bfloat16)
    w_buf[:, block(blk)] = weighted
    live = lax.broadcasted_iota(jnp.int32, (1, slots), 1) < count[...]
    own_strength = jnp.where(live, coef[...], 0.0)
    strength[...] = own_strength

    pl.semaphore_wait(barrier, nblk)
    mine = w_buf.at[:, block(blk)]
    gathers = [to_blk(mine, mine, gather_sem, blk, peer) for peer in peers]
    for copy in gathers:
        copy.start()
    asks = [to_other(second, asked, ask_sem, 0), to_other(strength, asked_strength, ask_sem, 1)]
    for copy in asks:
        copy.start()

    cell_in = lax.broadcasted_iota(jnp.int32, (BUILD_ROWS, slots), 0)

    def mark(cells, part):
        def build(step, carry):
            base = pl.multiple_of(step * BUILD_ROWS, BUILD_ROWS)
            one = jnp.where(cell_in == cells - base, 1.0, 0.0)
            hot[pl.ds(base, BUILD_ROWS), pl.ds(part * slots, slots)] = one.astype(jnp.bfloat16)
            return carry

        lax.fori_loop(0, part_cells // BUILD_ROWS, build, 0)

    second_row = second[...]
    mark(first[...], 0)
    mark(second_row, 1)
    for k in range(CHUNKS):
        loads[k].wait()
        p_own[:, rows(k)] = mxu(weighted, s_buf[rows(k), block(blk)], NT)
    for copy in asks:
        copy.wait_recv()
    mark(asked[...] - part_cells, 2)
    val_own[...] = mxu(weighted, hot[block(blk), :])

    swaps = []
    for place, peer in enumerate(peers):
        theirs = w_buf.at[:, block(peer)]
        to_blk(theirs, theirs, gather_sem, peer, peer).wait_recv()
        cols = w_buf[:, block(peer)]
        value = val_own[...] + mxu(cols, hot[block(peer), :])
        if place < nblk - 2:
            val_own[...] = value
        else:
            first_val = value[:, :slots]
            second_val = value[:, slots : 2 * slots]
            answer = value[:, 2 * slots :]
            val_send[...] = jnp.concatenate([first_val, answer], axis=1).astype(jnp.bfloat16)
            trade = to_other(val_send, val_recv, val_sem)
            trade.start()
        for k in range(CHUNKS):
            partial = p_own[:, rows(k)] + mxu(cols, s_buf[rows(k), block(peer)], NT)
            p_own[:, rows(k)] = partial
            if place == nblk - 2:
                p_send[k] = partial.astype(jnp.bfloat16)
                swap = to_other(p_send.at[k], p_recv.at[k], p_sem, k)
                swap.start()
                swaps.append(swap)

    def residual_of(k):
        predicted = p_own[:, rows(k)] + p_recv[k].astype(jnp.float32)
        factor = jnp.concatenate(
            [weight[pl.ds(k * per_chunk + i, 1), :] for i in range(per_chunk)], axis=1
        )
        return (factor * predicted).astype(jnp.bfloat16)

    crossing = jnp.where(second_row >= part_cells, 1.0, 0.0)
    trade.wait_recv()
    jump = first_val - second_val - crossing * val_recv[:, slots:].astype(jnp.float32)
    flux = own_strength * (own_strength * jump)
    far_strength = jnp.where(asked[...] >= part_cells, asked_strength[...], 0.0)
    far_jump = val_recv[:, :slots].astype(jnp.float32) - answer
    far_flux = far_strength * (far_strength * far_jump)
    flux_pair = in_two(jnp.concatenate([flux, -flux, -far_flux], axis=1))
    spread = mxu(flux_pair, hot[...], NT)
    spread = spread[:probe_count] + spread[probe_count:]
    acc[...] = spread
    for copy in swaps:
        copy.wait_recv()
    late = jnp.concatenate([residual_of(k) for k in range(CHUNKS)], axis=1)
    late_rows = pl.ds(0, CHUNKS * chunk_rows)
    sums = []
    for place, peer in enumerate(reversed(peers)):
        term = acc[:, block(peer)] + mxu(late, s_buf[late_rows, block(peer)])
        part_send[place] = term.astype(jnp.bfloat16)
        copy = to_blk(part_send.at[place], part_recv.at[blk], part_sem, blk, peer)
        copy.start()
        sums.append(copy)
    total = acc[:, block(blk)] + mxu(late, s_buf[late_rows, block(blk)])
    for peer in peers:
        theirs = part_recv.at[peer]
        to_blk(theirs, theirs, part_sem, peer, peer).wait_recv()
        total = total + part_recv[peer].astype(jnp.float32)
    out[...] = total * scale

    for copy in gathers + asks + [trade] + swaps + sums:
        copy.wait_send()


def hand_on(value, out):
    out[:, 0, :] = value[...]


def fused_form(
    nblk,
    probes,
    depth_level,
    depth_scale,
    sensitivity,
    data_weight,
    face_first,
    face_second,
    face_coef,
    face_count,
):
    probe_count, _, own_cells = probes.shape
    comps, stations, _, part_cells = sensitivity.shape
    rows = comps * stations
    slots = face_first.shape[1]
    matrix = sensitivity[:, :, 0, :].reshape(rows, part_cells)
    vmem = pl.BlockSpec(memory_space=pltpu.VMEM)
    bf16, f32, i32 = jnp.bfloat16, jnp.float32, jnp.int32
    dma = pltpu.SemaphoreType.DMA
    result = pl.pallas_call(
        fused_kernel,
        out_shape=jax.ShapeDtypeStruct((probe_count, own_cells), f32),
        in_specs=[pl.BlockSpec(memory_space=pltpu.HBM)] * 9,
        out_specs=vmem,
        scratch_shapes=[
            pltpu.VMEM((probe_count, own_cells), bf16),
            pltpu.VMEM((1, own_cells), i32),
            pltpu.SMEM(depth_scale.shape, f32),
            pltpu.VMEM((comps, stations), f32),
            pltpu.VMEM((1, slots), i32),
            pltpu.VMEM((1, slots), i32),
            pltpu.VMEM((1, slots), f32),
            pltpu.VMEM((1, 1), i32),
            pltpu.VMEM((rows, part_cells), bf16),
            pltpu.VMEM((probe_count, part_cells), bf16),
            pltpu.VMEM((part_cells, 3 * slots), bf16),
            pltpu.VMEM((1, slots), f32),
            pltpu.VMEM((1, slots), i32),
            pltpu.VMEM((1, slots), f32),
            pltpu.VMEM((probe_count, 2 * slots), bf16),
            pltpu.VMEM((probe_count, 2 * slots), bf16),
            pltpu.VMEM((probe_count, 3 * slots), f32),
            pltpu.VMEM((probe_count, rows), f32),
            pltpu.VMEM((CHUNKS, probe_count, rows // CHUNKS), bf16),
            pltpu.VMEM((CHUNKS, probe_count, rows // CHUNKS), bf16),
            pltpu.VMEM((probe_count, part_cells), f32),
            pltpu.VMEM((nblk - 1, probe_count, own_cells), bf16),
            pltpu.VMEM((nblk, probe_count, own_cells), bf16),
            dma((8,)),
            dma((CHUNKS,)),
            dma((2, 2)),
            dma((2, nblk)),
            dma((2, 1)),
            dma((2, CHUNKS)),
            dma((2, nblk)),
        ],
        compiler_params=pltpu.CompilerParams(
            collective_id=0, has_side_effects=True, vmem_limit_bytes=56 * 2**20
        ),
        cost_estimate=pl.CostEstimate(
            flops=4 * probe_count * rows * part_cells,
            bytes_accessed=2 * rows * part_cells,
            transcendentals=0,
        ),
    )(
        probes[:, 0, :],
        depth_level,
        depth_scale,
        matrix,
        data_weight,
        face_first,
        face_second,
        face_coef,
        face_count,
    )
    return pl.pallas_call(
        hand_on,
        out_shape=jax.ShapeDtypeStruct((probe_count, 1, own_cells), f32),
        in_specs=[vmem],
        out_specs=vmem,
    )(result)


def fits_kernel(nblk, ncells, probes, sensitivity):
    own_cells = probes.shape[2]
    comps, stations, _, part_cells = sensitivity.shape
    return (
        nblk == 4
        and ncells == 2
        and own_cells % 128 == 0
        and part_cells % BUILD_ROWS == 0
        and stations % 128 == 0
        and comps % CHUNKS == 0
        and probes.shape[0] % 16 == 0
    )


def on_device(nblk, ncells, *arrays):
    if fits_kernel(nblk, ncells, arrays[0], arrays[3]):
        return fused_form(nblk, *arrays)
    return plain_form(*arrays)


def solution(mesh):
    return jax.shard_map(
        functools.partial(on_device, mesh.shape["blk"], mesh.shape["cells"]),
        mesh=mesh,
        in_specs=(
            P("rep", "cells", ("groups", "blk")),
            P("cells", ("groups", "blk")),
            P(),
            P(None, ("groups", "blk"), "cells", None),
            P(None, ("groups", "blk")),
            P("cells", ("groups", "blk")),
            P("cells", ("groups", "blk")),
            P("cells", ("groups", "blk")),
            P("cells", ("groups", "blk")),
        ),
        out_specs=P("rep", "cells", ("groups", "blk")),
        check_vma=False,
    )
```
